256 devices in a mesh: dp: 4 (over y), ctx: 64 (over x, z, core).
Axes of the slice: x: 4, y: 4, z: 8, core: 2. Of those that a mesh axis runs over, the one named last changes fastest.
Arguments:
- queries: bfloat16 [4, 16384, 16, 128], P('dp', 'ctx'), may hold values from -64 to 64
- keys: bfloat16 [4, 16384, 8, 128], P('dp', 'ctx'), may hold values from -64 to 64
- values: bfloat16 [4, 16384, 8, 128], P('dp', 'ctx'), may hold values from -6 to 6
- out_grad: bfloat16 [4, 16384, 16, 128], P('dp', 'ctx'), may hold values from -8 to 8
- segment_ids: int32 [4, 16384], P('dp'), may hold values from 0 to 7, never falling along the last dimension, each value on 1 to 4096 neighbouring positions
- query_gain: float32 [128], replicated, may hold values from 0.5 to 6.5
- key_gain: float32 [128], replicated, may hold values from 0.5 to 6.5
Outputs:
- attention_out: bfloat16 [4, 16384, 16, 128], P('dp', 'ctx')
- query_grad: bfloat16 [4, 16384, 16, 128], P('dp', 'ctx')
- key_grad: bfloat16 [4, 16384, 8, 128], P('dp', 'ctx')
- value_grad: bfloat16 [4, 16384, 8, 128], P('dp', 'ctx')
- query_gain_grad: float32 [128], replicated
- key_gain_grad: float32 [128], replicated
The draws below stay inside these ranges and needn't reach their ends.
All inputs are finite; a program needn't handle non-finite values.
Results may differ from the reference program's by a relative error of at most 0.034.
The reference program's roundings to bfloat16 on the way count: a program that leaves them out, or rounds other values in their place, can miss the bound.
Values may be sent and summed in bfloat16 or wider, within the bound.
A program may use at most 128 MiB of HBM per device.

```python
import math
import jax
import jax.numpy as jnp
import numpy as np
from jax import lax

QUERY_HEADS = 16
KEY_VALUE_HEADS = 8
HEAD_SIZE = 128
LOOKBACK_TOKENS = 1024
TOK_DEV = 256
PACKED_SEQUENCES = 4
PACKED_LENGTH = 16384
DOCS = 8
DOC_MOST = 4096


def scaled_queries(key, widened_heads):
    leading_part, second, third_part = jax.random.split(key, 3)
    unscaled_scores = jax.random.normal(leading_part, (PACKED_SEQUENCES, PACKED_LENGTH, QUERY_HEADS, HEAD_SIZE), jnp.float32)
    row_span = jnp.exp(jax.random.uniform(second, (PACKED_SEQUENCES, PACKED_LENGTH, 1, 1), minval=0.0, maxval=widened_heads))
    column_span = jnp.exp(jax.random.uniform(third_part, (1, 1, QUERY_HEADS, HEAD_SIZE), minval=0.0, maxval=widened_heads))
    return unscaled_scores * row_span * column_span


def draw_queries(key, part):
    widened_heads = 0.0
    return jnp.clip(scaled_queries(key, widened_heads), -64.0, 64.0).astype(jnp.bfloat16)


def draw_keys(key, part):
    widened_heads = 0.0
    key = jax.random.fold_in(key, 3)
    leading_part, second, third_part = jax.random.split(key, 3)
    unscaled_scores = jax.random.normal(leading_part, (PACKED_SEQUENCES, PACKED_LENGTH, KEY_VALUE_HEADS, HEAD_SIZE), jnp.float32)
    row_span = jnp.exp(jax.random.uniform(second, (PACKED_SEQUENCES, PACKED_LENGTH, 1, 1), minval=0.0, maxval=widened_heads))
    column_span = jnp.exp(jax.random.uniform(third_part, (1, 1, KEY_VALUE_HEADS, HEAD_SIZE), minval=0.0, maxval=widened_heads))
    unscaled_scores = unscaled_scores * row_span * column_span
    return jnp.clip(unscaled_scores, -64.0, 64.0).astype(jnp.bfloat16)


def draw_out_grad(key, part):
    key = jax.random.fold_in(key, 7)
    leading_part = jax.random.fold_in(key, 0)
    place = (jnp.arange(PACKED_LENGTH, dtype=jnp.float32) / PACKED_LENGTH)[None, :, None, None]
    result = (0.5 + place) * jax.random.normal(leading_part, (PACKED_SEQUENCES, PACKED_LENGTH, QUERY_HEADS, HEAD_SIZE), jnp.float32)
    return jnp.clip(result, -8.0, 8.0).astype(jnp.bfloat16)


def draw_query_gain(key, part):
    key = jax.random.fold_in(key, 5)
    return jax.random.uniform(key, (HEAD_SIZE,), minval=0.5, maxval=2.0)


def draw_key_gain(key, part):
    key = jax.random.fold_in(key, 9)
    return jax.random.uniform(key, (HEAD_SIZE,), minval=0.5, maxval=2.0)


def levels(own_key, shape, pieces, smallest, largest):
    def one(axis_at, shards_of):
        draws = jax.random.uniform(jax.random.fold_in(jax.random.fold_in(own_key, 6), axis_at), (shards_of,), jnp.float32, smallest / len(pieces), largest / len(pieces))
        return jnp.repeat(jnp.exp(draws), shape[axis_at] // shards_of).reshape((-1,) + (1,) * (len(shape) - axis_at - 1))

    level = one(*pieces[0])
    for cut in pieces[1:]:
        level = level * one(*cut)
    return level


def profile(number_of, total, most, slope):
    loads = [(1 << 20) // math.isqrt(grade ** slope) + 1 for grade in range(2, number_of + 1)]
    spare, counts = total - most - (number_of - 1), [1] * (number_of - 1)
    while spare > 0:
        movable = [i for i in range(number_of - 1) if counts[i] < most]
        mass, left = sum([loads[i] for i in movable]), spare
        for i in movable:
            extra = min(most - counts[i], max(1, left * loads[i] // mass), spare)
            counts[i] = counts[i] + extra
            spare = spare - extra
    return np.array([most] + counts)


def ragged(own_key, amount, total, reach, skew):
    if amount == 2:
        one = jax.random.randint(own_key, (), max(1, total - reach), min(reach, total - 1) + 1)
        return jnp.stack([one, total - one])
    tallies = jnp.asarray(profile(amount, total, reach, skew), jnp.int32)
    twos = (amount - 1) // 2
    source_of, receiver = tallies[1:1 + 2 * twos:2], tallies[2:2 + 2 * twos:2]
    room = jnp.minimum(source_of - 1, reach - receiver)
    moved = jax.random.randint(jax.random.fold_in(own_key, 1), (twos,), 0, 1 << 20) % (room + 1)
    tallies = tallies.at[1:1 + 2 * twos:2].set(source_of - moved).at[2:2 + 2 * twos:2].set(receiver + moved)
    return tallies[jax.random.permutation(jax.random.fold_in(own_key, 2), amount)]


def noise(key, dims, scale, limit, shards=(), held_as=jnp.bfloat16):
    entries = scale * jax.random.normal(key, dims, jnp.float32)
    if shards:
        entries = entries * levels(key, dims, shards, -0.22, 0.18)
    return jnp.clip(entries, -limit, limit).astype(held_as)


def setup_inputs(seed: int = 0) -> dict:
    key_list = jax.random.split(jax.random.key(seed), 8)
    return {
        "queries": draw_queries(jax.random.fold_in(key_list[7], 71), 0),
        "keys": draw_keys(jax.random.fold_in(key_list[7], 71), 0),
        "values": noise(key_list[2], (PACKED_SEQUENCES, PACKED_LENGTH, KEY_VALUE_HEADS, HEAD_SIZE), 1.0, 6.0, ((0, 4), (1, 64))),
        "out_grad": draw_out_grad(jax.random.fold_in(key_list[7], 71), 0),
        "segment_ids": jax.vmap(lambda own: jnp.searchsorted(jnp.cumsum(ragged(own, DOCS, PACKED_LENGTH, DOC_MOST, 2)), jnp.arange(PACKED_LENGTH), side="right"))(jax.random.split(key_list[4], PACKED_SEQUENCES)).reshape((PACKED_SEQUENCES, PACKED_LENGTH)).astype(jnp.int32),
        "query_gain": draw_query_gain(jax.random.fold_in(key_list[7], 71), 0),
        "key_gain": draw_key_gain(jax.random.fold_in(key_list[7], 71), 0),
    }


score_scale = 168.0 ** (-0.5)
eps = 1e-06

def normalize(unscaled_scores, gain):
    values = unscaled_scores.astype(jnp.float32)
    factor = lax.rsqrt(lax.optimization_barrier(jnp.mean(values * values, axis=-1, keepdims=True)) + eps)
    unit = values * factor
    return (unit, factor, (unit * gain).astype(jnp.bfloat16))

def norm_backward(grad, unit, factor, gain):
    scaled = grad * gain
    inner = lax.optimization_barrier(jnp.mean(scaled * unit, axis=-1, keepdims=True))
    return ((factor * (scaled - unit * inner)).astype(jnp.bfloat16), lax.optimization_barrier(jnp.sum(grad * unit, axis=(0, 1))))

def head_block(query_group, key_rows, value_row_slice, grad_group, allowed):
    wide = jnp.float32
    scores = jnp.einsum('tgc,kc->gtk', query_group.astype(wide), key_rows.astype(wide)) * score_scale
    scores = jnp.where(allowed[None], scores, -jnp.inf)
    top = lax.optimization_barrier(jnp.max(scores, axis=-1, keepdims=True))
    lse = top + jnp.log(lax.optimization_barrier(jnp.sum(jnp.exp(scores - top), axis=-1, keepdims=True)))
    probs = jnp.exp(scores - lse)
    rounded = probs.astype(jnp.bfloat16)
    output = jnp.einsum('gtk,kc->tgc', rounded.astype(wide), value_row_slice.astype(wide)).astype(jnp.bfloat16)
    dprob = jnp.einsum('tgc,kc->gtk', grad_group.astype(wide), value_row_slice.astype(wide))
    delta = jnp.einsum('tgc,tgc->gt', grad_group.astype(wide), output.astype(wide))
    dscore = (probs * (dprob - delta[..., None])).astype(jnp.bfloat16)
    dquery = jnp.einsum('gtk,kc->tgc', dscore.astype(wide), key_rows.astype(wide)) * score_scale
    dkey = jnp.einsum('gtk,tgc->kc', dscore.astype(wide), query_group.astype(wide)) * score_scale
    dvalue = jnp.einsum('gtk,tgc->kc', rounded.astype(wide), grad_group.astype(wide))
    return (output, dquery, dkey, dvalue)

def round_earlier(term):
    earlier = lax.optimization_barrier(term[:LOOKBACK_TOKENS].astype(jnp.bfloat16)).astype(jnp.float32)
    return jnp.concatenate([earlier, term[LOOKBACK_TOKENS:]], axis=0)

def reference(queries, keys, values, out_grad, segment_ids, query_gain, key_gain):
    row_span = TOK_DEV
    query_cluster = QUERY_HEADS // KEY_VALUE_HEADS
    blocks = PACKED_LENGTH // row_span
    mapped = jax.vmap(head_block, in_axes=(1, 1, 1, 1, None), out_axes=(1, 1, 1, 1))

    def one_sequence(operands):
        query_raw, key_raw, value_row_slice, gradient_rows, segments = operands
        query_unit, query_factor, normalized_query = normalize(query_raw, query_gain)
        key_unit, key_factor, normalized_key = normalize(key_raw, key_gain)
        key_with_margin = jnp.concatenate([jnp.zeros((LOOKBACK_TOKENS, KEY_VALUE_HEADS, HEAD_SIZE), jnp.bfloat16), normalized_key], axis=0)
        value_with_margin = jnp.concatenate([jnp.zeros((LOOKBACK_TOKENS, KEY_VALUE_HEADS, HEAD_SIZE), jnp.bfloat16), value_row_slice], axis=0)
        seg_padded = jnp.concatenate([jnp.full((LOOKBACK_TOKENS,), -1, jnp.int32), segments.astype(jnp.int32)], axis=0)
        query_pos = jnp.arange(row_span, dtype=jnp.int32)
        key_pos = jnp.arange(LOOKBACK_TOKENS + row_span, dtype=jnp.int32) - LOOKBACK_TOKENS

        def step(carry, block):
            dkey_acc, dvalue_acc = carry
            start_offset = (block * row_span).astype(jnp.int32)
            query_tile_block = lax.dynamic_slice_in_dim(normalized_query, start_offset, row_span, 0).reshape(row_span, KEY_VALUE_HEADS, query_cluster, HEAD_SIZE)
            gradient_block = lax.dynamic_slice_in_dim(gradient_rows, start_offset, row_span, 0).reshape(row_span, KEY_VALUE_HEADS, query_cluster, HEAD_SIZE)
            key_block = lax.dynamic_slice_in_dim(key_with_margin, start_offset, LOOKBACK_TOKENS + row_span, 0)
            value_block = lax.dynamic_slice_in_dim(value_with_margin, start_offset, LOOKBACK_TOKENS + row_span, 0)
            seg_query = lax.dynamic_slice_in_dim(segments.astype(jnp.int32), start_offset, row_span, 0)
            seg_key = lax.dynamic_slice_in_dim(seg_padded, start_offset, LOOKBACK_TOKENS + row_span, 0)
            offset = query_pos[:, None] - key_pos[None, :]
            allowed = (offset >= 0) & (offset < LOOKBACK_TOKENS) & (seg_query[:, None] == seg_key[None, :])
            output, dquery, dkey, dvalue = mapped(query_tile_block, key_block, value_block, gradient_block, allowed)
            dkey = round_earlier(dkey)
            dvalue = round_earlier(dvalue)
            old_key = lax.dynamic_slice_in_dim(dkey_acc, start_offset, LOOKBACK_TOKENS + row_span, 0)
            old_value = lax.dynamic_slice_in_dim(dvalue_acc, start_offset, LOOKBACK_TOKENS + row_span, 0)
            dkey_acc = lax.dynamic_update_slice_in_dim(dkey_acc, old_key + dkey, start_offset, 0)
            dvalue_acc = lax.dynamic_update_slice_in_dim(dvalue_acc, old_value + dvalue, start_offset, 0)
            return ((dkey_acc, dvalue_acc), (output.reshape(row_span, QUERY_HEADS, HEAD_SIZE), dquery.reshape(row_span, QUERY_HEADS, HEAD_SIZE)))
        zero_margin = jnp.zeros((LOOKBACK_TOKENS + PACKED_LENGTH, KEY_VALUE_HEADS, HEAD_SIZE), jnp.float32)
        (dkey_acc, dvalue_acc), (outputs, dqueries) = lax.scan(step, (zero_margin, zero_margin), jnp.arange(blocks, dtype=jnp.int32))
        output = outputs.reshape(PACKED_LENGTH, QUERY_HEADS, HEAD_SIZE)
        dquery_normed = dqueries.reshape(PACKED_LENGTH, QUERY_HEADS, HEAD_SIZE)
        dkey_normed = dkey_acc[LOOKBACK_TOKENS:]
        query_grad, query_part = norm_backward(dquery_normed, query_unit, query_factor, query_gain)
        key_grad, key_part = norm_backward(dkey_normed, key_unit, key_factor, key_gain)
        return (output, query_grad, key_grad, dvalue_acc[LOOKBACK_TOKENS:].astype(jnp.bfloat16), query_part, key_part)
    output, query_grad, key_grad, value_grad, query_parts, key_parts = lax.map(one_sequence, (queries, keys, values, out_grad, segment_ids))
    return (output, query_grad, key_grad, value_grad, lax.optimization_barrier(jnp.sum(query_parts, axis=0)), lax.optimization_barrier(jnp.sum(key_parts, axis=0)))
```

```python
import jax
import jax.numpy as jnp
from jax import lax
from jax.experimental import pallas as pl
from jax.experimental.pallas import tpu as pltpu
from jax.sharding import PartitionSpec as P

LOOKBACK_TOKENS = 1024
BLOCK = 256
WIDTH = 128
SPAN = 6
score_scale = 168.0 ** (-0.5)
log2_scale = score_scale * 1.4426950408889634
eps = 1e-06
HIDDEN = -1e30
AHEAD = 3

MESH = pl.DeviceIdType.MESH
NT = (((1,), (1,)), ((), ()))
TN = (((0,), (0,)), ((), ()))
NN = (((1,), (0,)), ((), ()))


def dot(a, b, dims):
    return lax.dot_general(a, b, dims, preferred_element_type=jnp.float32)


def rows(block):
    return pl.ds(pl.multiple_of(block * BLOCK, BLOCK), BLOCK)


def normalize(raw, gain):
    wide = raw.astype(jnp.float32)
    factor = lax.rsqrt(jnp.mean(wide * wide, axis=-1, keepdims=True) + eps)
    unit = wide * factor
    return unit, factor, (unit * gain).astype(jnp.bfloat16)


def norm_backward(grad, unit, factor, gain):
    scaled = grad * gain
    inner = jnp.mean(scaled * unit, axis=-1, keepdims=True)
    return (factor * (scaled - unit * inner)).astype(jnp.bfloat16), jnp.sum(
        grad * unit, axis=0, keepdims=True
    )


def kernel(
    q_ref, k_ref, v_ref, g_ref, seg_key, seg_query, gain_ref,
    o_ref, dq_ref, dk_ref, dv_ref, part_ref,
    kv, q_all, g_all, mask, s_buf, d_buf, p_bf, ds_bf, o_buf, dq_buf,
    held, pair_out, pair_in, a_out, a_in, b_out, b_in,
    one_send, one_recv, sends, recvs,
):
    dp = lax.axis_index("dp")
    me = lax.axis_index("ctx")
    count = lax.axis_size("ctx")
    core = lax.rem(me, 2)
    other = 1 - core
    sibling = (dp, me + 1 - 2 * core)
    after = (dp, lax.rem(me + 2, count))
    before = (dp, lax.rem(me + count - 2, count))
    heads = k_ref.shape[0]

    def remote(src, dst, kind, head, device):
        return pltpu.make_async_remote_copy(
            src_ref=src, dst_ref=dst, send_sem=sends.at[kind, head], recv_sem=recvs.at[kind, head],
            device_id=device, device_id_type=MESH,
        )

    def own_to_after(h):
        return remote(kv.at[h, :, rows(4 + core)], kv.at[h, :, rows(2 + core)], 0, h, after)

    def pass_on(h):
        return remote(kv.at[h, :, rows(2 + core)], kv.at[h, :, rows(core)], 1, h, after)

    def share_near(h):
        return remote(kv.at[h, :, rows(2 + core)], kv.at[h, :, rows(2 + core)], 2, h, sibling)

    def share_far(h):
        return remote(kv.at[h, :, rows(core)], kv.at[h, :, rows(core)], 3, h, sibling)

    def output_to_sibling(h):
        return remote(o_buf.at[h, other], o_ref.at[h, core], 4, h, sibling)

    def dquery_to_sibling(h):
        return remote(dq_buf.at[h, other], dq_ref.at[h, core], 5, h, sibling)

    def terms_to_sibling(h):
        return remote(pair_out.at[h], pair_in.at[h], 6, h, sibling)

    def far_terms(h):
        return remote(a_out.at[h], a_in.at[h], 7, h, before)

    def near_terms(h):
        return remote(b_out.at[h], b_in.at[h], 8, h, before)

    def single(src, dst, index):
        return pltpu.make_async_remote_copy(
            src_ref=src, dst_ref=dst, send_sem=one_send.at[index], recv_sem=one_recv.at[index],
            device_id=sibling, device_id_type=MESH,
        )

    own_to_sibling = single(kv.at[:, :, rows(4 + core)], kv.at[:, :, rows(4 + core)], 0)
    query_to_sibling = single(q_ref.at[:, other], q_all.at[:, rows(core)], 1)
    grad_to_sibling = single(g_ref.at[:, other], g_all.at[:, rows(core)], 2)

    query_gain = gain_ref[0:1]
    key_gain = gain_ref[1:2]

    def fill(h, carry):
        kv[h, 0, rows(4 + core)] = normalize(k_ref[h], key_gain)[2]
        kv[h, 1, rows(4 + core)] = v_ref[h]
        return carry

    lax.fori_loop(0, heads, fill, 0)

    barrier = pltpu.get_barrier_semaphore()
    for device in (sibling, after, before):
        pl.semaphore_signal(barrier, inc=1, device_id=device, device_id_type=MESH)
    pl.semaphore_wait(barrier, 3)

    for h in range(AHEAD):
        own_to_after(h).start()
    own_to_sibling.start()
    query_to_sibling.start()
    grad_to_sibling.start()

    part_ref[...] = jnp.zeros_like(part_ref)
    p_bf[...] = jnp.zeros_like(p_bf)
    ds_bf[...] = jnp.zeros_like(ds_bf)
    for h in range(heads):
        q_all[h, rows(core)] = q_ref[h, core]
        g_all[h, rows(core)] = g_ref[h, core]
    for qb in range(2):
        for kb in range(qb, qb + 5):
            behind = (
                (4 + qb - kb) * BLOCK
                + lax.broadcasted_iota(jnp.int32, (BLOCK, BLOCK), 1)
                - lax.broadcasted_iota(jnp.int32, (BLOCK, BLOCK), 0)
            )
            allowed = (
                (behind >= 0)
                & (behind < LOOKBACK_TOKENS)
                & (seg_key[pl.ds(kb * BLOCK, BLOCK)] == seg_query[:, pl.ds(qb * BLOCK, BLOCK)])
            )
            mask[pl.ds(kb * BLOCK, BLOCK), pl.ds(qb * BLOCK, BLOCK)] = jnp.where(
                allowed, 0.0, HIDDEN
            )

    def arrive_near(h):
        own_to_after(h).wait_recv()
        pass_on(h).start()
        share_near(h).start()

    for h in range(AHEAD):
        arrive_near(h)
        own_to_after(h + AHEAD).start()
    own_to_sibling.wait_recv()
    query_to_sibling.wait_recv()
    grad_to_sibling.wait_recv()

    def attend(h):
        query_unit, query_factor, query_normed = normalize(q_all[h], query_gain)
        grad = g_all[h]
        part = jnp.zeros((1, WIDTH), jnp.float32)
        for qb in range(2):
            columns = slice(qb * BLOCK, (qb + 1) * BLOCK)
            top = None
            for i in range(5):
                kb = pl.ds((qb + i) * BLOCK, BLOCK)
                scores = (
                    dot(kv[h, 0, kb], query_normed[columns], NT) * log2_scale + mask[kb, columns]
                )
                s_buf[qb, i] = scores
                tile_top = jnp.max(scores, axis=0, keepdims=True)
                top = tile_top if top is None else jnp.maximum(top, tile_top)
            total = jnp.zeros((1, BLOCK), jnp.float32)
            inner = jnp.zeros((1, BLOCK), jnp.float32)
            for i in range(5):
                kb = pl.ds((qb + i) * BLOCK, BLOCK)
                dprob = dot(kv[h, 1, kb], grad[columns], NT)
                weight = jnp.exp2(s_buf[qb, i] - top)
                s_buf[qb, i] = weight
                d_buf[qb, i] = dprob
                total = total + jnp.sum(weight, axis=0, keepdims=True)
                inner = inner + jnp.sum(weight * dprob, axis=0, keepdims=True)
            inverse = 1.0 / total
            delta = inner * inverse
            for i in range(5):
                kb = pl.ds((qb + i) * BLOCK, BLOCK)
                probs = s_buf[qb, i] * inverse
                p_bf[kb, columns] = probs.astype(jnp.bfloat16)
                ds_bf[kb, columns] = (probs * (d_buf[qb, i] - delta)).astype(jnp.bfloat16)
            window = pl.ds(qb * BLOCK, 5 * BLOCK)
            o_buf[h, qb] = dot(kv[h, 1, window], p_bf[window, columns], TN).T.astype(jnp.bfloat16)
            dquery = dot(kv[h, 0, window], ds_bf[window, columns], TN).T * score_scale
            dq_buf[h, qb], gain_part = norm_backward(
                dquery, query_unit[columns], query_factor[columns], query_gain
            )
            part = part + gain_part
        part_ref[0:1] += part
        for chip in range(3):
            kb = rows(2 * chip + other)
            dkey = dot(ds_bf[kb], query_normed, NN) * score_scale
            pair_out[h, chip, 0] = dkey.astype(jnp.bfloat16)
            pair_out[h, chip, 1] = dot(p_bf[kb], grad, NN).astype(jnp.bfloat16)
        terms_to_sibling(h).start()
        for chip in range(3):
            kb = rows(2 * chip + core)
            held[h, chip, 0] = dot(ds_bf[kb], query_normed, NN) * score_scale
            held[h, chip, 1] = dot(p_bf[kb], grad, NN)
        output_to_sibling(h).start()
        dquery_to_sibling(h).start()
        o_ref[h, core] = o_buf[h, core]
        dq_ref[h, core] = dq_buf[h, core]

    def step(s, carry):
        @pl.when(s < heads)
        def _():
            pass_on(s).wait_recv()
            share_far(s).start()
            share_near(s).wait_recv()
            share_far(s).wait_recv()
            attend(s)

        @pl.when(s + AHEAD < heads)
        def _():
            arrive_near(s + AHEAD)

        @pl.when(s + 2 * AHEAD < heads)
        def _():
            own_to_after(s + 2 * AHEAD).start()

        @pl.when((s >= 1) & (s < heads + 1))
        def _():
            h = s - 1
            terms_to_sibling(h).wait_recv()
            a_out[h] = (held[h, 0] + pair_in[h, 0].astype(jnp.float32)).astype(jnp.bfloat16)
            far_terms(h).start()

        @pl.when((s >= 2) & (s < heads + 2))
        def _():
            h = s - 2
            far_terms(h).wait_recv()
            b_out[h] = (
                held[h, 1] + pair_in[h, 1].astype(jnp.float32) + a_in[h].astype(jnp.float32)
            ).astype(jnp.bfloat16)
            near_terms(h).start()

        @pl.when(s >= 3)
        def _():
            h = s - 3
            near_terms(h).wait_recv()
            term = held[h, 2] + pair_in[h, 2].astype(jnp.float32) + b_in[h].astype(jnp.float32)
            key_unit, key_factor, _ = normalize(k_ref[h], key_gain)
            dk_ref[h], gain_part = norm_backward(term[0], key_unit, key_factor, key_gain)
            dv_ref[h] = term[1].astype(jnp.bfloat16)
            part_ref[1:2] += gain_part

        return carry

    lax.fori_loop(0, heads + 3, step, 0)

    def finish(h, carry):
        output_to_sibling(h).wait_recv()
        dquery_to_sibling(h).wait_recv()
        for copy in (
            own_to_after, pass_on, share_near, share_far, output_to_sibling, dquery_to_sibling,
            terms_to_sibling, far_terms, near_terms,
        ):
            copy(h).wait_send()
        return carry

    lax.fori_loop(0, heads, finish, 0)
    own_to_sibling.wait_send()
    query_to_sibling.wait_send()
    grad_to_sibling.wait_send()


def attention(q, k, v, g, seg_key, seg_query, gains):
    groups = k.shape[0]
    half = jnp.bfloat16
    wide = jnp.float32
    vmem = pl.BlockSpec(memory_space=pltpu.VMEM)
    dma = pltpu.SemaphoreType.DMA
    return pl.pallas_call(
        kernel,
        out_shape=[
            jax.ShapeDtypeStruct((groups, 2, BLOCK, WIDTH), half),
            jax.ShapeDtypeStruct((groups, 2, BLOCK, WIDTH), half),
            jax.ShapeDtypeStruct((groups, BLOCK, WIDTH), half),
            jax.ShapeDtypeStruct((groups, BLOCK, WIDTH), half),
            jax.ShapeDtypeStruct((2, WIDTH), wide),
        ],
        in_specs=[vmem] * 7,
        out_specs=[vmem] * 5,
        scratch_shapes=[
            pltpu.VMEM((groups, 2, SPAN * BLOCK, WIDTH), half),
            pltpu.VMEM((groups, 2 * BLOCK, WIDTH), half),
            pltpu.VMEM((groups, 2 * BLOCK, WIDTH), half),
            pltpu.VMEM((SPAN * BLOCK, 2 * BLOCK), wide),
            pltpu.VMEM((2, 5, BLOCK, BLOCK), wide),
            pltpu.VMEM((2, 5, BLOCK, BLOCK), wide),
            pltpu.VMEM((SPAN * BLOCK, 2 * BLOCK), half),
            pltpu.VMEM((SPAN * BLOCK, 2 * BLOCK), half),
            pltpu.VMEM((groups, 2, BLOCK, WIDTH), half),
            pltpu.VMEM((groups, 2, BLOCK, WIDTH), half),
            pltpu.VMEM((groups, 3, 2, BLOCK, WIDTH), wide),
            pltpu.VMEM((groups, 3, 2, BLOCK, WIDTH), half),
            pltpu.VMEM((groups, 3, 2, BLOCK, WIDTH), half),
            pltpu.VMEM((groups, 2, BLOCK, WIDTH), half),
            pltpu.VMEM((groups, 2, BLOCK, WIDTH), half),
            pltpu.VMEM((groups, 2, BLOCK, WIDTH), half),
            pltpu.VMEM((groups, 2, BLOCK, WIDTH), half),
            dma((3,)),
            dma((3,)),
            dma((9, groups)),
            dma((9, groups)),
        ],
        compiler_params=pltpu.CompilerParams(
            collective_id=0, has_side_effects=True, vmem_limit_bytes=58 * 2**20
        ),
        name="attention",
    )(q, k, v, g, seg_key, seg_query, gains)


def local(queries, keys, values, out_grad, segment_ids, query_gain, key_gain):
    tokens, heads, width = queries.shape[1:]
    groups = keys.shape[2]
    position = lax.axis_index("ctx")
    chip = position // 2
    segments = segment_ids[0]
    padded = jnp.concatenate([jnp.full((4 * tokens,), -1, jnp.int32), segments], axis=0)
    window = lax.dynamic_slice_in_dim(padded, chip * 2 * tokens, SPAN * tokens, 0)
    by_head = lambda array: jnp.swapaxes(array[0], 0, 1)
    pairs = lambda array: by_head(array).reshape(groups, heads // groups, tokens, width)
    output, query_grad, key_grad, value_grad, part = attention(
        pairs(queries), by_head(keys), by_head(values), pairs(out_grad),
        window[:, None], window[None, 4 * tokens :], jnp.stack([query_gain, key_gain]),
    )
    total = lax.psum(part, ("dp", "ctx"))
    by_token = lambda array: jnp.swapaxes(array.reshape(-1, tokens, width), 0, 1)[None]
    return (
        by_token(output), by_token(query_grad), by_token(key_grad), by_token(value_grad),
        total[0], total[1],
    )


def solution(mesh):
    block = P("dp", "ctx", None, None)
    return jax.shard_map(
        local, mesh=mesh,
        in_specs=(block, block, block, block, P("dp", None), P(), P()),
        out_specs=(block, block, block, block, P(), P()),
        check_vma=False,
    )
```

```python
import jax
import jax.numpy as jnp
from jax import lax
from jax.experimental import pallas as pl
from jax.experimental.pallas import tpu as pltpu
from jax.sharding import PartitionSpec as P

LOOKBACK_TOKENS = 1024
BLOCK = 256
WIDTH = 128
SPAN = 6
score_scale = 168.0 ** (-0.5)
log2_scale = score_scale * 1.4426950408889634
eps = 1e-06
HIDDEN = -1e30
CHIPS_ALONG_Z = 8
AHEAD = 2

MESH = pl.DeviceIdType.MESH
NT = (((1,), (1,)), ((), ()))
TN = (((0,), (0,)), ((), ()))
NN = (((1,), (0,)), ((), ()))


def dot(a, b, dims):
    return lax.dot_general(a, b, dims, preferred_element_type=jnp.float32)


def rows(block):
    return pl.ds(pl.multiple_of(block * BLOCK, BLOCK), BLOCK)


def normalize(raw, gain):
    wide = raw.astype(jnp.float32)
    factor = lax.rsqrt(jnp.mean(wide * wide, axis=-1, keepdims=True) + eps)
    unit = wide * factor
    return unit, factor, (unit * gain).astype(jnp.bfloat16)


def norm_backward(grad, unit, factor, gain):
    scaled = grad * gain
    inner = jnp.mean(scaled * unit, axis=-1, keepdims=True)
    return (factor * (scaled - unit * inner)).astype(jnp.bfloat16), jnp.sum(
        grad * unit, axis=0, keepdims=True
    )


def kernel(
    q_hbm, k_hbm, v_hbm, g_hbm, seg_ref, gain_q, gain_k,
    o_hbm, dq_hbm, dk_hbm, dv_hbm, total_ref,
    q_in, k_in, v_in, g_in, wide, q_own, g_own,
    kv, q_all, g_all, mask, s_buf, d_buf, p_bf, ds_bf, key_bf, key_unit, o_buf, dq_buf,
    o_in, dq_in, held, pair_out, pair_in, a_out, a_in, b_out, b_in,
    o_wide, dq_wide, dk_wide, dv_wide, part, part_in, z_part, x_part, y_part,
    local_sem, one_send, one_recv, sends, recvs, sum_send, sum_recv,
):
    dp = lax.axis_index("dp")
    me = lax.axis_index("ctx")
    count = lax.axis_size("ctx")
    line = 2 * CHIPS_ALONG_Z
    columns_of_x = count // line
    sequences = lax.axis_size("dp")
    core = lax.rem(me, 2)
    other = 1 - core
    chip = me // 2
    z_at = lax.rem(chip, CHIPS_ALONG_Z)
    x_at = me // line
    sibling = (dp, me + 1 - 2 * core)
    after = (dp, lax.rem(me + 2, count))
    before = (dp, lax.rem(me + count - 2, count))
    heads = kv.shape[0]

    def along_z(d):
        return (dp, x_at * line + 2 * lax.rem(z_at + d, CHIPS_ALONG_Z) + core)

    def along_x(d):
        return (dp, lax.rem(me + d * line, count))

    def along_y(d):
        return (lax.rem(dp + d, sequences), me)

    barrier = pltpu.get_barrier_semaphore()
    friends = [sibling, after, before]
    friends += [along_z(d) for d in range(1, CHIPS_ALONG_Z)]
    friends += [along_x(d) for d in range(1, columns_of_x)]
    friends += [along_y(d) for d in range(1, sequences)]
    for device in friends:
        pl.semaphore_signal(barrier, inc=1, device_id=device, device_id_type=MESH)

    loads = [
        pltpu.make_async_copy(src, dst, local_sem.at[i])
        for i, (src, dst) in enumerate(
            ((k_hbm, k_in), (v_hbm, v_in), (q_hbm, q_in), (g_hbm, g_in))
        )
    ]
    for load in loads:
        load.start()

    def remote(src, dst, kind, head, device):
        return pltpu.make_async_remote_copy(
            src_ref=src, dst_ref=dst, send_sem=sends.at[kind, head], recv_sem=recvs.at[kind, head],
            device_id=device, device_id_type=MESH,
        )

    def own_to_after(h):
        return remote(kv.at[h, :, rows(4 + core)], kv.at[h, :, rows(2 + core)], 0, h, after)

    def pass_on(h):
        return remote(kv.at[h, :, rows(2 + core)], kv.at[h, :, rows(core)], 1, h, after)

    def share_near(h):
        return remote(kv.at[h, :, rows(2 + core)], kv.at[h, :, rows(2 + core)], 2, h, sibling)

    def share_far(h):
        return remote(kv.at[h, :, rows(core)], kv.at[h, :, rows(core)], 3, h, sibling)

    def output_to_sibling(h):
        return remote(o_buf.at[h, other], o_in.at[h], 4, h, sibling)

    def dquery_to_sibling(h):
        return remote(dq_buf.at[h, other], dq_in.at[h], 5, h, sibling)

    def terms_to_sibling(h):
        return remote(pair_out.at[h], pair_in.at[h], 6, h, sibling)

    def far_terms(h):
        return remote(a_out.at[h], a_in.at[h], 7, h, before)

    def near_terms(h):
        return remote(b_out.at[h], b_in.at[h], 8, h, before)

    def single(src, dst, index):
        return pltpu.make_async_remote_copy(
            src_ref=src, dst_ref=dst, send_sem=one_send.at[index], recv_sem=one_recv.at[index],
            device_id=sibling, device_id_type=MESH,
        )

    own_to_sibling = single(kv.at[:, :, rows(4 + core)], kv.at[:, :, rows(4 + core)], 0)
    query_to_sibling = single(q_own.at[:, other], q_all.at[:, rows(core)], 1)
    grad_to_sibling = single(g_own.at[:, other], g_all.at[:, rows(core)], 2)
    part_to_sibling = single(part, part_in, 3)

    def spread(ref, slot, index, device):
        return pltpu.make_async_remote_copy(
            src_ref=ref.at[slot], dst_ref=ref.at[slot],
            send_sem=sum_send.at[index], recv_sem=sum_recv.at[index],
            device_id=device, device_id_type=MESH,
        )

    z_sums = [spread(z_part, z_at, d, along_z(d)) for d in range(1, CHIPS_ALONG_Z)]
    x_sums = [
        spread(x_part, x_at, CHIPS_ALONG_Z + d, along_x(d)) for d in range(1, columns_of_x)
    ]
    y_sums = [
        spread(y_part, dp, CHIPS_ALONG_Z + columns_of_x + d, along_y(d))
        for d in range(1, sequences)
    ]
    query_gain = gain_q[...]
    key_gain = gain_k[...]

    def widen(ref):
        tokens, across, width = ref.shape
        wide[pl.ds(0, tokens * across)] = (
            ref[...].astype(jnp.float32).reshape(tokens * across, width)
        )

    def head_of(h, across):
        return wide[pl.ds(h, BLOCK, stride=across)].astype(jnp.bfloat16)

    loads[0].wait()
    widen(k_in)
    for h in range(heads):
        kv[h, 0, rows(4 + core)] = head_of(h, heads)
    loads[1].wait()
    widen(v_in)
    for h in range(heads):
        kv[h, 1, rows(4 + core)] = head_of(h, heads)

    pl.semaphore_wait(barrier, len(friends))

    for h in range(AHEAD):
        own_to_after(h).start()
    own_to_sibling.start()

    for load, source, own, everything, copy in (
        (loads[2], q_in, q_own, q_all, query_to_sibling),
        (loads[3], g_in, g_own, g_all, grad_to_sibling),
    ):
        load.wait()
        widen(source)
        for h in range(heads):
            for pair in range(2):
                own[h, pair] = head_of(2 * h + pair, 2 * heads)
        copy.start()
        for h in range(heads):
            everything[h, rows(core)] = own[h, core]

    part[...] = jnp.zeros_like(part)
    corner = jnp.zeros((BLOCK, BLOCK), jnp.bfloat16)
    for ref in (p_bf, ds_bf):
        ref[pl.ds(0, BLOCK), pl.ds(BLOCK, BLOCK)] = corner
        ref[pl.ds(5 * BLOCK, BLOCK), pl.ds(0, BLOCK)] = corner

    def arrive_near(h):
        own_to_after(h).wait_recv()
        pass_on(h).start()
        share_near(h).start()

    arrive_near(0)
    own_to_after(AHEAD).start()

    def segments_of(block):
        place = jnp.maximum(2 * chip - 4 + block, 0) * BLOCK
        found = seg_ref[0:1, pl.ds(pl.multiple_of(place, BLOCK), BLOCK)].astype(jnp.float32)
        return jnp.where(2 * chip - 4 + block >= 0, found, -1.0)

    for kb in range(SPAN):
        by_key = jnp.broadcast_to(segments_of(kb), (WIDTH, BLOCK)).T
        for qb in range(2):
            if not qb <= kb < qb + 5:
                continue
            by_query = segments_of(4 + qb)
            for part_at in range(0, BLOCK, WIDTH):
                behind = (
                    (4 + qb - kb) * BLOCK
                    + part_at
                    + lax.broadcasted_iota(jnp.int32, (BLOCK, WIDTH), 1)
                    - lax.broadcasted_iota(jnp.int32, (BLOCK, WIDTH), 0)
                )
                allowed = (
                    (behind >= 0)
                    & (behind < LOOKBACK_TOKENS)
                    & (by_key == by_query[:, part_at : part_at + WIDTH])
                )
                mask[pl.ds(kb * BLOCK, BLOCK), pl.ds(qb * BLOCK + part_at, WIDTH)] = jnp.where(
                    allowed, 0.0, HIDDEN
                )

    for h in range(1, AHEAD):
        arrive_near(h)
        own_to_after(h + AHEAD).start()
    own_to_sibling.wait_recv()
    query_to_sibling.wait_recv()
    grad_to_sibling.wait_recv()

    def attend(h):
        query_unit, query_factor, query_normed = normalize(q_all[h], query_gain)
        key_unit[...], _, key_bf[...] = normalize(kv[h, 0], key_gain)
        grad = g_all[h]
        for qb in range(2):
            columns = slice(qb * BLOCK, (qb + 1) * BLOCK)
            top = None
            for i in range(5):
                kb = pl.ds((qb + i) * BLOCK, BLOCK)
                scores = dot(key_bf[kb], query_normed[columns], NT) * log2_scale + mask[kb, columns]
                s_buf[qb, i] = scores
                tile_top = jnp.max(scores, axis=0, keepdims=True)
                top = tile_top if top is None else jnp.maximum(top, tile_top)
            total = jnp.zeros((1, BLOCK), jnp.float32)
            inner = jnp.zeros((1, BLOCK), jnp.float32)
            for i in range(5):
                kb = pl.ds((qb + i) * BLOCK, BLOCK)
                dprob = dot(kv[h, 1, kb], grad[columns], NT)
                weight = jnp.exp2(s_buf[qb, i] - top)
                s_buf[qb, i] = weight
                d_buf[qb, i] = dprob
                total = total + jnp.sum(weight, axis=0, keepdims=True)
                inner = inner + jnp.sum(weight * dprob, axis=0, keepdims=True)
            inverse = 1.0 / total
            delta = inner * inverse
            for i in range(5):
                kb = pl.ds((qb + i) * BLOCK, BLOCK)
                probs = s_buf[qb, i] * inverse
                p_bf[kb, columns] = probs.astype(jnp.bfloat16)
                ds_bf[kb, columns] = (probs * (d_buf[qb, i] - delta)).astype(jnp.bfloat16)
        key_part = jnp.zeros((1, WIDTH), jnp.float32)
        for near in range(3):
            kb = rows(2 * near + other)
            dkey = dot(ds_bf[kb], query_normed, NN) * score_scale
            pair_out[h, near, 0] = dkey.astype(jnp.bfloat16)
            pair_out[h, near, 1] = dot(p_bf[kb], grad, NN).astype(jnp.bfloat16)
            key_part = key_part + jnp.sum(dkey * key_unit[kb], axis=0, keepdims=True)
        terms_to_sibling(h).start()
        for near in range(3):
            kb = rows(2 * near + core)
            dkey = dot(ds_bf[kb], query_normed, NN) * score_scale
            held[h, near, 0] = dkey
            held[h, near, 1] = dot(p_bf[kb], grad, NN)
            key_part = key_part + jnp.sum(dkey * key_unit[kb], axis=0, keepdims=True)
        query_part = jnp.zeros((1, WIDTH), jnp.float32)
        for qb in range(2):
            columns = slice(qb * BLOCK, (qb + 1) * BLOCK)
            window = pl.ds(qb * BLOCK, 5 * BLOCK)
            dquery = dot(key_bf[window], ds_bf[window, columns], TN).T * score_scale
            dq_buf[h, qb], gain_part = norm_backward(
                dquery, query_unit[columns], query_factor[columns], query_gain
            )
            query_part = query_part + gain_part
            o_buf[h, qb] = dot(kv[h, 1, window], p_bf[window, columns], TN).T.astype(jnp.bfloat16)
        part[0:1] += query_part
        part[1:2] += key_part
        dquery_to_sibling(h).start()
        output_to_sibling(h).start()

    def send_far(h):
        terms_to_sibling(h).wait_recv()
        a_out[h] = (held[h, 0] + pair_in[h, 0].astype(jnp.float32)).astype(jnp.bfloat16)
        far_terms(h).start()

    def send_near(h):
        far_terms(h).wait_recv()
        b_out[h] = (
            held[h, 1] + pair_in[h, 1].astype(jnp.float32) + a_in[h].astype(jnp.float32)
        ).astype(jnp.bfloat16)
        near_terms(h).start()

    def finish_key(h):
        near_terms(h).wait_recv()
        term = held[h, 2] + pair_in[h, 2].astype(jnp.float32) + b_in[h].astype(jnp.float32)
        unit, factor, _ = normalize(kv[h, 0, rows(4 + core)], key_gain)
        grad, _ = norm_backward(term[0], unit, factor, key_gain)
        dk_wide[pl.ds(h, BLOCK, stride=heads)] = grad.astype(jnp.float32)
        dv_wide[pl.ds(h, BLOCK, stride=heads)] = term[1]

    def step(s, carry):
        pass_on(s).wait_recv()
        share_far(s).start()
        share_near(s).wait_recv()
        share_far(s).wait_recv()
        attend(s)

        @pl.when(s + AHEAD < heads)
        def _():
            arrive_near(s + AHEAD)

        @pl.when(s + 2 * AHEAD < heads)
        def _():
            own_to_after(s + 2 * AHEAD).start()

        @pl.when(s >= 1)
        def _():
            send_far(s - 1)

        @pl.when(s >= 2)
        def _():
            send_near(s - 2)

        @pl.when(s >= 3)
        def _():
            finish_key(s - 3)

        return carry

    lax.fori_loop(0, heads, step, 0)

    part_to_sibling.start()
    send_far(heads - 1)
    part_to_sibling.wait_recv()
    z_part[z_at] = part[...] + part_in[...]
    for copy in z_sums:
        copy.start()
    send_near(heads - 2)
    finish_key(heads - 3)

    def natural(into, ours, theirs, h):
        into[pl.ds(2 * h + core, BLOCK, stride=2 * heads)] = ours[h, core].astype(jnp.float32)
        into[pl.ds(2 * h + other, BLOCK, stride=2 * heads)] = theirs[h].astype(jnp.float32)

    def narrow(into, ref):
        tokens, across, width = into.shape
        into[...] = ref[...].reshape(tokens, across, width).astype(jnp.bfloat16)

    for h in range(heads):
        dquery_to_sibling(h).wait_recv()
        output_to_sibling(h).wait_recv()
        natural(dq_wide, dq_buf, dq_in, h)
        natural(o_wide, o_buf, o_in, h)
    send_near(heads - 1)
    for copy in z_sums:
        copy.wait_recv()
    x_part[x_at] = jnp.sum(z_part[...], axis=0)
    for copy in x_sums:
        copy.start()
    finish_key(heads - 2)
    narrow(q_in, dq_wide)
    stores = [pltpu.make_async_copy(q_in, dq_hbm, local_sem.at[0])]
    stores[0].start()
    for copy in x_sums:
        copy.wait_recv()
    y_part[dp] = jnp.sum(x_part[...], axis=0)
    for copy in y_sums:
        copy.start()
    narrow(g_in, o_wide)
    stores.append(pltpu.make_async_copy(g_in, o_hbm, local_sem.at[1]))
    stores[1].start()
    finish_key(heads - 1)
    narrow(k_in, dk_wide)
    stores.append(pltpu.make_async_copy(k_in, dk_hbm, local_sem.at[2]))
    stores[2].start()
    narrow(v_in, dv_wide)
    stores.append(pltpu.make_async_copy(v_in, dv_hbm, local_sem.at[3]))
    stores[3].start()
    for copy in y_sums:
        copy.wait_recv()
    total_ref[...] = jnp.sum(y_part[...], axis=0)

    def sent(h, carry):
        for copy in (
            own_to_after, pass_on, share_near, share_far, output_to_sibling, dquery_to_sibling,
            terms_to_sibling, far_terms, near_terms,
        ):
            copy(h).wait_send()
        return carry

    lax.fori_loop(0, heads, sent, 0)
    for copy in (own_to_sibling, query_to_sibling, grad_to_sibling, part_to_sibling):
        copy.wait_send()
    for copy in z_sums + x_sums + y_sums:
        copy.wait_send()
    for store in stores:
        store.wait()


def attention(q, k, v, g, segments, gain_q, gain_k, sequences, columns_of_x):
    tokens, groups, width = k.shape
    half = jnp.bfloat16
    wide = jnp.float32
    vmem = pl.BlockSpec(memory_space=pltpu.VMEM)
    anywhere = pl.BlockSpec(memory_space=pl.ANY)
    dma = pltpu.SemaphoreType.DMA
    sums = CHIPS_ALONG_Z + columns_of_x + sequences
    return pl.pallas_call(
        kernel,
        out_shape=[
            jax.ShapeDtypeStruct(q.shape, half),
            jax.ShapeDtypeStruct(q.shape, half),
            jax.ShapeDtypeStruct(k.shape, half),
            jax.ShapeDtypeStruct(k.shape, half),
            jax.ShapeDtypeStruct((8, width), wide),
        ],
        in_specs=[anywhere] * 4 + [vmem] * 3,
        out_specs=[anywhere] * 4 + [vmem],
        scratch_shapes=[
            pltpu.VMEM(q.shape, half),
            pltpu.VMEM(k.shape, half),
            pltpu.VMEM(k.shape, half),
            pltpu.VMEM(q.shape, half),
            pltpu.VMEM((2 * groups * tokens, width), wide),
            pltpu.VMEM((groups, 2, tokens, width), half),
            pltpu.VMEM((groups, 2, tokens, width), half),
            pltpu.VMEM((groups, 2, SPAN * tokens, width), half),
            pltpu.VMEM((groups, 2 * tokens, width), half),
            pltpu.VMEM((groups, 2 * tokens, width), half),
            pltpu.VMEM((SPAN * tokens, 2 * tokens), wide),
            pltpu.VMEM((2, 5, tokens, tokens), wide),
            pltpu.VMEM((2, 5, tokens, tokens), wide),
            pltpu.VMEM((SPAN * tokens, 2 * tokens), half),
            pltpu.VMEM((SPAN * tokens, 2 * tokens), half),
            pltpu.VMEM((SPAN * tokens, width), half),
            pltpu.VMEM((SPAN * tokens, width), wide),
            pltpu.VMEM((groups, 2, tokens, width), half),
            pltpu.VMEM((groups, 2, tokens, width), half),
            pltpu.VMEM((groups, tokens, width), half),
            pltpu.VMEM((groups, tokens, width), half),
            pltpu.VMEM((groups, 3, 2, tokens, width), wide),
            pltpu.VMEM((groups, 3, 2, tokens, width), half),
            pltpu.VMEM((groups, 3, 2, tokens, width), half),
            pltpu.VMEM((groups, 2, tokens, width), half),
            pltpu.VMEM((groups, 2, tokens, width), half),
            pltpu.VMEM((groups, 2, tokens, width), half),
            pltpu.VMEM((groups, 2, tokens, width), half),
            pltpu.VMEM((2 * groups * tokens, width), wide),
            pltpu.VMEM((2 * groups * tokens, width), wide),
            pltpu.VMEM((groups * tokens, width), wide),
            pltpu.VMEM((groups * tokens, width), wide),
            pltpu.VMEM((8, width), wide),
            pltpu.VMEM((8, width), wide),
            pltpu.VMEM((CHIPS_ALONG_Z, 8, width), wide),
            pltpu.VMEM((columns_of_x, 8, width), wide),
            pltpu.VMEM((sequences, 8, width), wide),
            dma((4,)),
            dma((4,)),
            dma((4,)),
            dma((9, groups)),
            dma((9, groups)),
            dma((sums,)),
            dma((sums,)),
        ],
        compiler_params=pltpu.CompilerParams(
            collective_id=0, has_side_effects=True, vmem_limit_bytes=60 * 2**20
        ),
        name="attention",
    )(q, k, v, g, segments, gain_q, gain_k)


def local(queries, keys, values, out_grad, segment_ids, query_gain, key_gain):
    sequences = lax.axis_size("dp")
    columns_of_x = lax.axis_size("ctx") // (2 * CHIPS_ALONG_Z)
    output, query_grad, key_grad, value_grad, total = attention(
        queries[0], keys[0], values[0], out_grad[0], segment_ids,
        query_gain[None], key_gain[None], sequences, columns_of_x,
    )
    return (
        output[None], query_grad[None], key_grad[None], value_grad[None], total[0], total[1],
    )


def solution(mesh):
    block = P("dp", "ctx", None, None)
    return jax.shard_map(
        local, mesh=mesh,
        in_specs=(block, block, block, block, P("dp", None), P(), P()),
        out_specs=(block, block, block, block, P(), P()),
        check_vma=False,
    )
```

```python
import jax
import jax.numpy as jnp
from jax import lax
from jax.experimental import pallas as pl
from jax.experimental.pallas import tpu as pltpu
from jax.sharding import PartitionSpec as P

LOOKBACK_TOKENS = 1024
BLOCK = 256
WIDTH = 128
SPAN = 6
score_scale = 168.0 ** (-0.5)
log2_scale = score_scale * 1.4426950408889634
eps = 1e-06
HIDDEN = -1e30
CHIPS_ALONG_Z = 8
AHEAD = 2

MESH = pl.DeviceIdType.MESH
NT = (((1,), (1,)), ((), ()))
TN = (((0,), (0,)), ((), ()))
NN = (((1,), (0,)), ((), ()))


def dot(a, b, dims):
    return lax.dot_general(a, b, dims, preferred_element_type=jnp.float32)


def rows(block):
    return pl.ds(pl.multiple_of(block * BLOCK, BLOCK), BLOCK)


def normalize(raw, gain):
    wide = raw.astype(jnp.float32)
    factor = lax.rsqrt(jnp.mean(wide * wide, axis=-1, keepdims=True) + eps)
    unit = wide * factor
    return unit, factor, (unit * gain).astype(jnp.bfloat16)


def norm_backward(grad, unit, factor, gain):
    scaled = grad * gain
    inner = jnp.mean(scaled * unit, axis=-1, keepdims=True)
    return (factor * (scaled - unit * inner)).astype(jnp.bfloat16), jnp.sum(
        grad * unit, axis=0, keepdims=True
    )


def kernel(
    q_hbm, k_hbm, v_hbm, g_hbm, seg_ref, gain_q, gain_k,
    o_hbm, dq_hbm, dk_hbm, dv_hbm, total_ref,
    q_in, k_in, v_in, g_in, wide, q_own, g_own,
    kv, q_all, g_all, mask, s_buf, d_buf, p_bf, ds_bf, key_own, o_buf, dq_buf,
    o_in, dq_in, held, pair_out, pair_in, a_out, a_in, b_out, b_in,
    o_wide, dq_wide, dk_wide, dv_wide, part, part_in, z_part, x_part, y_part,
    local_sem, one_send, one_recv, sends, recvs, sum_send, sum_recv,
):
    dp = lax.axis_index("dp")
    me = lax.axis_index("ctx")
    count = lax.axis_size("ctx")
    line = 2 * CHIPS_ALONG_Z
    columns_of_x = count // line
    sequences = lax.axis_size("dp")
    core = lax.rem(me, 2)
    other = 1 - core
    chip = me // 2
    z_at = lax.rem(chip, CHIPS_ALONG_Z)
    x_at = me // line
    sibling = (dp, me + 1 - 2 * core)
    after = (dp, lax.rem(me + 2, count))
    before = (dp, lax.rem(me + count - 2, count))
    heads = kv.shape[0]

    def along_z(d):
        return (dp, x_at * line + 2 * lax.rem(z_at + d, CHIPS_ALONG_Z) + core)

    def along_x(d):
        return (dp, lax.rem(me + d * line, count))

    def along_y(d):
        return (lax.rem(dp + d, sequences), me)

    barrier = pltpu.get_barrier_semaphore()
    friends = [sibling, after, before]
    friends += [along_z(d) for d in range(1, CHIPS_ALONG_Z)]
    friends += [along_x(d) for d in range(1, columns_of_x)]
    friends += [along_y(d) for d in range(1, sequences)]
    for device in friends:
        pl.semaphore_signal(barrier, inc=1, device_id=device, device_id_type=MESH)

    loads = [
        pltpu.make_async_copy(src, dst, local_sem.at[i])
        for i, (src, dst) in enumerate(
            ((k_hbm, k_in), (v_hbm, v_in), (q_hbm, q_in), (g_hbm, g_in))
        )
    ]
    for load in loads:
        load.start()

    def remote(src, dst, kind, head, device):
        return pltpu.make_async_remote_copy(
            src_ref=src, dst_ref=dst, send_sem=sends.at[kind, head], recv_sem=recvs.at[kind, head],
            device_id=device, device_id_type=MESH,
        )

    def own_to_after(h):
        return remote(kv.at[h, :, rows(4 + core)], kv.at[h, :, rows(2 + core)], 0, h, after)

    def pass_on(h):
        return remote(kv.at[h, :, rows(2 + core)], kv.at[h, :, rows(core)], 1, h, after)

    def share_near(h):
        return remote(kv.at[h, :, rows(2 + core)], kv.at[h, :, rows(2 + core)], 2, h, sibling)

    def share_far(h):
        return remote(kv.at[h, :, rows(core)], kv.at[h, :, rows(core)], 3, h, sibling)

    def output_to_sibling(h):
        return remote(o_buf.at[h, other], o_in.at[h], 4, h, sibling)

    def dquery_to_sibling(h):
        return remote(dq_buf.at[h, other], dq_in.at[h], 5, h, sibling)

    def terms_to_sibling(h):
        return remote(pair_out.at[h], pair_in.at[h], 6, h, sibling)

    def far_terms(h):
        return remote(a_out.at[h], a_in.at[h], 7, h, before)

    def near_terms(h):
        return remote(b_out.at[h], b_in.at[h], 8, h, before)

    def single(src, dst, index):
        return pltpu.make_async_remote_copy(
            src_ref=src, dst_ref=dst, send_sem=one_send.at[index], recv_sem=one_recv.at[index],
            device_id=sibling, device_id_type=MESH,
        )

    own_to_sibling = single(kv.at[:, :, rows(4 + core)], kv.at[:, :, rows(4 + core)], 0)
    query_to_sibling = single(q_own.at[:, other], q_all.at[:, rows(core)], 1)
    grad_to_sibling = single(g_own.at[:, other], g_all.at[:, rows(core)], 2)
    part_to_sibling = single(part, part_in, 3)

    def spread(ref, slot, index, device):
        return pltpu.make_async_remote_copy(
            src_ref=ref.at[slot], dst_ref=ref.at[slot],
            send_sem=sum_send.at[index], recv_sem=sum_recv.at[index],
            device_id=device, device_id_type=MESH,
        )

    z_sums = [spread(z_part, z_at, d, along_z(d)) for d in range(1, CHIPS_ALONG_Z)]
    x_sums = [
        spread(x_part, x_at, CHIPS_ALONG_Z + d, along_x(d)) for d in range(1, columns_of_x)
    ]
    y_sums = [
        spread(y_part, dp, CHIPS_ALONG_Z + columns_of_x + d, along_y(d))
        for d in range(1, sequences)
    ]
    query_gain = gain_q[...]
    key_gain = gain_k[...]

    def widen(ref):
        tokens, across, width = ref.shape
        wide[pl.ds(0, tokens * across)] = (
            ref[...].astype(jnp.float32).reshape(tokens * across, width)
        )

    def head_of(h, across):
        return wide[pl.ds(h, BLOCK, stride=across)].astype(jnp.bfloat16)

    loads[0].wait()
    widen(k_in)
    for h in range(heads):
        key_own[h] = head_of(h, heads)
        kv[h, 0, rows(4 + core)] = normalize(key_own[h], key_gain)[2]
    loads[1].wait()
    widen(v_in)
    for h in range(heads):
        kv[h, 1, rows(4 + core)] = head_of(h, heads)

    pl.semaphore_wait(barrier, len(friends))

    for h in range(AHEAD):
        own_to_after(h).start()
    own_to_sibling.start()

    for load, source, own, everything, copy in (
        (loads[2], q_in, q_own, q_all, query_to_sibling),
        (loads[3], g_in, g_own, g_all, grad_to_sibling),
    ):
        load.wait()
        widen(source)
        for h in range(heads):
            for pair in range(2):
                own[h, pair] = head_of(2 * h + pair, 2 * heads)
        copy.start()
        for h in range(heads):
            everything[h, rows(core)] = own[h, core]

    part[...] = jnp.zeros_like(part)
    corner = jnp.zeros((BLOCK, BLOCK), jnp.bfloat16)
    for ref in (p_bf, ds_bf):
        ref[pl.ds(0, BLOCK), pl.ds(BLOCK, BLOCK)] = corner
        ref[pl.ds(5 * BLOCK, BLOCK), pl.ds(0, BLOCK)] = corner

    def arrive_near(h):
        own_to_after(h).wait_recv()
        pass_on(h).start()
        share_near(h).start()

    arrive_near(0)
    own_to_after(AHEAD).start()

    def segments_of(block):
        place = jnp.maximum(2 * chip - 4 + block, 0) * BLOCK
        found = seg_ref[0:1, pl.ds(pl.multiple_of(place, BLOCK), BLOCK)].astype(jnp.float32)
        return jnp.where(2 * chip - 4 + block >= 0, found, -1.0)

    for kb in range(SPAN):
        by_key = jnp.broadcast_to(segments_of(kb), (WIDTH, BLOCK)).T
        for qb in range(2):
            if not qb <= kb < qb + 5:
                continue
            by_query = segments_of(4 + qb)
            for part_at in range(0, BLOCK, WIDTH):
                behind = (
                    (4 + qb - kb) * BLOCK
                    + part_at
                    + lax.broadcasted_iota(jnp.int32, (BLOCK, WIDTH), 1)
                    - lax.broadcasted_iota(jnp.int32, (BLOCK, WIDTH), 0)
                )
                allowed = (
                    (behind >= 0)
                    & (behind < LOOKBACK_TOKENS)
                    & (by_key == by_query[:, part_at : part_at + WIDTH])
                )
                mask[pl.ds(kb * BLOCK, BLOCK), pl.ds(qb * BLOCK + part_at, WIDTH)] = jnp.where(
                    allowed, 0.0, HIDDEN
                )

    for h in range(1, AHEAD):
        arrive_near(h)
        own_to_after(h + AHEAD).start()
    own_to_sibling.wait_recv()
    query_to_sibling.wait_recv()
    grad_to_sibling.wait_recv()

    def attend(h):
        query_unit, query_factor, query_normed = normalize(q_all[h], query_gain)
        grad = g_all[h]
        for qb in range(2):
            columns = slice(qb * BLOCK, (qb + 1) * BLOCK)
            top = None
            for i in range(5):
                kb = pl.ds((qb + i) * BLOCK, BLOCK)
                scores = dot(kv[h, 0, kb], query_normed[columns], NT) * log2_scale + mask[kb, columns]
                s_buf[qb, i] = scores
                tile_top = jnp.max(scores, axis=0, keepdims=True)
                top = tile_top if top is None else jnp.maximum(top, tile_top)
            total = jnp.zeros((1, BLOCK), jnp.float32)
            inner = jnp.zeros((1, BLOCK), jnp.float32)
            for i in range(5):
                kb = pl.ds((qb + i) * BLOCK, BLOCK)
                dprob = dot(kv[h, 1, kb], grad[columns], NT)
                weight = jnp.exp2(s_buf[qb, i] - top)
                s_buf[qb, i] = weight
                d_buf[qb, i] = dprob
                total = total + jnp.sum(weight, axis=0, keepdims=True)
                inner = inner + jnp.sum(weight * dprob, axis=0, keepdims=True)
            inverse = 1.0 / total
            delta = inner * inverse
            for i in range(5):
                kb = pl.ds((qb + i) * BLOCK, BLOCK)
                probs = s_buf[qb, i] * inverse
                p_bf[kb, columns] = probs.astype(jnp.bfloat16)
                ds_bf[kb, columns] = (probs * (d_buf[qb, i] - delta)).astype(jnp.bfloat16)
        key_part = jnp.zeros((1, WIDTH), jnp.float32)
        for near in range(3):
            kb = rows(2 * near + other)
            dkey = dot(ds_bf[kb], query_normed, NN) * score_scale
            pair_out[h, near, 0] = dkey.astype(jnp.bfloat16)
            pair_out[h, near, 1] = dot(p_bf[kb], grad, NN).astype(jnp.bfloat16)
            key_part = key_part + jnp.sum(
                dkey * kv[h, 0, kb].astype(jnp.float32), axis=0, keepdims=True
            )
        terms_to_sibling(h).start()
        for near in range(3):
            kb = rows(2 * near + core)
            dkey = dot(ds_bf[kb], query_normed, NN) * score_scale
            held[h, near, 0] = dkey
            held[h, near, 1] = dot(p_bf[kb], grad, NN)
            key_part = key_part + jnp.sum(
                dkey * kv[h, 0, kb].astype(jnp.float32), axis=0, keepdims=True
            )
        query_part = jnp.zeros((1, WIDTH), jnp.float32)
        for qb in range(2):
            columns = slice(qb * BLOCK, (qb + 1) * BLOCK)
            window = pl.ds(qb * BLOCK, 5 * BLOCK)
            dquery = dot(kv[h, 0, window], ds_bf[window, columns], TN).T * score_scale
            dq_buf[h, qb], gain_part = norm_backward(
                dquery, query_unit[columns], query_factor[columns], query_gain
            )
            query_part = query_part + gain_part
            o_buf[h, qb] = dot(kv[h, 1, window], p_bf[window, columns], TN).T.astype(jnp.bfloat16)
        part[0:1] += query_part
        part[1:2] += key_part / key_gain
        dquery_to_sibling(h).start()
        output_to_sibling(h).start()

    def send_far(h):
        terms_to_sibling(h).wait_recv()
        a_out[h] = (held[h, 0] + pair_in[h, 0].astype(jnp.float32)).astype(jnp.bfloat16)
        far_terms(h).start()

    def send_near(h):
        far_terms(h).wait_recv()
        b_out[h] = (
            held[h, 1] + pair_in[h, 1].astype(jnp.float32) + a_in[h].astype(jnp.float32)
        ).astype(jnp.bfloat16)
        near_terms(h).start()

    def finish_key(h):
        near_terms(h).wait_recv()
        term = held[h, 2] + pair_in[h, 2].astype(jnp.float32) + b_in[h].astype(jnp.float32)
        unit, factor, _ = normalize(key_own[h], key_gain)
        grad, _ = norm_backward(term[0], unit, factor, key_gain)
        dk_wide[pl.ds(h, BLOCK, stride=heads)] = grad.astype(jnp.float32)
        dv_wide[pl.ds(h, BLOCK, stride=heads)] = term[1]

    def step(s, carry):
        share_near(s).wait_recv()
        share_far(s).wait_recv()
        attend(s)

        @pl.when(s == heads - 1)
        def _():
            x_part[x_at] = part[...]
            for copy in x_sums:
                copy.start()

        send_far(s)

        @pl.when(s + AHEAD < heads)
        def _():
            arrive_near(s + AHEAD)

        @pl.when(s + 2 * AHEAD < heads)
        def _():
            own_to_after(s + 2 * AHEAD).start()

        @pl.when(s + 1 < heads)
        def _():
            pass_on(s + 1).wait_recv()
            share_far(s + 1).start()

        @pl.when(s >= 1)
        def _():
            send_near(s - 1)

        @pl.when(s >= 2)
        def _():
            finish_key(s - 2)

        return carry

    pass_on(0).wait_recv()
    share_far(0).start()
    lax.fori_loop(0, heads, step, 0)

    def natural(into, ours, theirs, h):
        into[pl.ds(2 * h + core, BLOCK, stride=2 * heads)] = ours[h, core].astype(jnp.float32)
        into[pl.ds(2 * h + other, BLOCK, stride=2 * heads)] = theirs[h].astype(jnp.float32)

    def narrow(into, ref):
        tokens, across, width = into.shape
        into[...] = ref[...].reshape(tokens, across, width).astype(jnp.bfloat16)

    for copy in x_sums:
        copy.wait_recv()
    y_part[dp] = jnp.sum(x_part[...], axis=0)
    for copy in y_sums:
        copy.start()
    for h in range(heads):
        dquery_to_sibling(h).wait_recv()
        natural(dq_wide, dq_buf, dq_in, h)
    for copy in y_sums:
        copy.wait_recv()
    part[...] = jnp.sum(y_part[...], axis=0)
    part_to_sibling.start()
    narrow(q_in, dq_wide)
    stores = [pltpu.make_async_copy(q_in, dq_hbm, local_sem.at[0])]
    stores[0].start()
    part_to_sibling.wait_recv()
    z_part[z_at] = part[...] + part_in[...]
    for copy in z_sums:
        copy.start()
    send_near(heads - 1)
    for h in range(heads):
        output_to_sibling(h).wait_recv()
        natural(o_wide, o_buf, o_in, h)
    narrow(g_in, o_wide)
    stores.append(pltpu.make_async_copy(g_in, o_hbm, local_sem.at[1]))
    stores[1].start()
    finish_key(heads - 2)
    for copy in z_sums:
        copy.wait_recv()
    total_ref[...] = jnp.sum(z_part[...], axis=0)
    finish_key(heads - 1)
    narrow(k_in, dk_wide)
    stores.append(pltpu.make_async_copy(k_in, dk_hbm, local_sem.at[2]))
    stores[2].start()
    narrow(v_in, dv_wide)
    stores.append(pltpu.make_async_copy(v_in, dv_hbm, local_sem.at[3]))
    stores[3].start()

    def sent(h, carry):
        for copy in (
            own_to_after, pass_on, share_near, share_far, output_to_sibling, dquery_to_sibling,
            terms_to_sibling, far_terms, near_terms,
        ):
            copy(h).wait_send()
        return carry

    lax.fori_loop(0, heads, sent, 0)
    for copy in (own_to_sibling, query_to_sibling, grad_to_sibling, part_to_sibling):
        copy.wait_send()
    for copy in z_sums + x_sums + y_sums:
        copy.wait_send()
    for store in stores:
        store.wait()


def attention(q, k, v, g, segments, gain_q, gain_k, sequences, columns_of_x):
    tokens, groups, width = k.shape
    half = jnp.bfloat16
    wide = jnp.float32
    vmem = pl.BlockSpec(memory_space=pltpu.VMEM)
    anywhere = pl.BlockSpec(memory_space=pl.ANY)
    dma = pltpu.SemaphoreType.DMA
    sums = CHIPS_ALONG_Z + columns_of_x + sequences
    return pl.pallas_call(
        kernel,
        out_shape=[
            jax.ShapeDtypeStruct(q.shape, half),
            jax.ShapeDtypeStruct(q.shape, half),
            jax.ShapeDtypeStruct(k.shape, half),
            jax.ShapeDtypeStruct(k.shape, half),
            jax.ShapeDtypeStruct((8, width), wide),
        ],
        in_specs=[anywhere] * 4 + [vmem] * 3,
        out_specs=[anywhere] * 4 + [vmem],
        scratch_shapes=[
            pltpu.VMEM(q.shape, half),
            pltpu.VMEM(k.shape, half),
            pltpu.VMEM(k.shape, half),
            pltpu.VMEM(q.shape, half),
            pltpu.VMEM((2 * groups * tokens, width), wide),
            pltpu.VMEM((groups, 2, tokens, width), half),
            pltpu.VMEM((groups, 2, tokens, width), half),
            pltpu.VMEM((groups, 2, SPAN * tokens, width), half),
            pltpu.VMEM((groups, 2 * tokens, width), half),
            pltpu.VMEM((groups, 2 * tokens, width), half),
            pltpu.VMEM((SPAN * tokens, 2 * tokens), wide),
            pltpu.VMEM((2, 5, tokens, tokens), wide),
            pltpu.VMEM((2, 5, tokens, tokens), wide),
            pltpu.VMEM((SPAN * tokens, 2 * tokens), half),
            pltpu.VMEM((SPAN * tokens, 2 * tokens), half),
            pltpu.VMEM((groups, tokens, width), half),
            pltpu.VMEM((groups, 2, tokens, width), half),
            pltpu.VMEM((groups, 2, tokens, width), half),
            pltpu.VMEM((groups, tokens, width), half),
            pltpu.VMEM((groups, tokens, width), half),
            pltpu.VMEM((groups, 3, 2, tokens, width), wide),
            pltpu.VMEM((groups, 3, 2, tokens, width), half),
            pltpu.VMEM((groups, 3, 2, tokens, width), half),
            pltpu.VMEM((groups, 2, tokens, width), half),
            pltpu.VMEM((groups, 2, tokens, width), half),
            pltpu.VMEM((groups, 2, tokens, width), half),
            pltpu.VMEM((groups, 2, tokens, width), half),
            pltpu.VMEM((2 * groups * tokens, width), wide),
            pltpu.VMEM((2 * groups * tokens, width), wide),
            pltpu.VMEM((groups * tokens, width), wide),
            pltpu.VMEM((groups * tokens, width), wide),
            pltpu.VMEM((8, width), wide),
            pltpu.VMEM((8, width), wide),
            pltpu.VMEM((CHIPS_ALONG_Z, 8, width), wide),
            pltpu.VMEM((columns_of_x, 8, width), wide),
            pltpu.VMEM((sequences, 8, width), wide),
            dma((4,)),
            dma((4,)),
            dma((4,)),
            dma((9, groups)),
            dma((9, groups)),
            dma((sums,)),
            dma((sums,)),
        ],
        compiler_params=pltpu.CompilerParams(
            collective_id=0, has_side_effects=True, vmem_limit_bytes=60 * 2**20
        ),
        name="attention",
    )(q, k, v, g, segments, gain_q, gain_k)


def deliver_kernel(
    o, dq, dk, dv, total, o_out, dq_out, dk_out, dv_out, gain_q, gain_k,
    o_held, dq_held, dk_held, dv_held, load_sem, store_sem,
):
    loads = []
    stores = []
    for src, held, dst, pieces in (
        (o, o_held, o_out, 4), (dq, dq_held, dq_out, 4),
        (dk, dk_held, dk_out, 2), (dv, dv_held, dv_out, 2),
    ):
        size = src.shape[0] // pieces
        for piece in range(pieces):
            span = pl.ds(piece * size, size)
            at = len(loads)
            loads.append(pltpu.make_async_copy(src.at[span], held.at[span], load_sem.at[at]))
            stores.append(pltpu.make_async_copy(held.at[span], dst.at[span], store_sem.at[at]))
    for load in loads:
        load.start()
    gain_q[...] = total[0:1]
    gain_k[...] = total[1:2]
    for load, store in zip(loads, stores):
        load.wait()
        store.start()
    for store in stores:
        store.wait()


def deliver(output, query_grad, key_grad, value_grad, total):
    vmem = pl.BlockSpec(memory_space=pltpu.VMEM)
    anywhere = pl.BlockSpec(memory_space=pl.ANY)
    arrays = (output, query_grad, key_grad, value_grad)
    gain = jax.ShapeDtypeStruct((1, total.shape[1]), total.dtype)
    return pl.pallas_call(
        deliver_kernel,
        out_shape=[jax.ShapeDtypeStruct(array.shape, array.dtype) for array in arrays] + [gain] * 2,
        in_specs=[anywhere] * 4 + [vmem],
        out_specs=[anywhere] * 4 + [vmem] * 2,
        scratch_shapes=[pltpu.VMEM(array.shape, array.dtype) for array in arrays]
        + [pltpu.SemaphoreType.DMA((12,))] * 2,
        name="deliver",
    )(*arrays, total)


def local(queries, keys, values, out_grad, segment_ids, query_gain, key_gain):
    sequences = lax.axis_size("dp")
    columns_of_x = lax.axis_size("ctx") // (2 * CHIPS_ALONG_Z)
    results = attention(
        queries[0], keys[0], values[0], out_grad[0], segment_ids,
        query_gain[None], key_gain[None], sequences, columns_of_x,
    )
    output, query_grad, key_grad, value_grad, query_total, key_total = deliver(*results)
    return (
        output[None], query_grad[None], key_grad[None], value_grad[None],
        query_total[0], key_total[0],
    )


def solution(mesh):
    block = P("dp", "ctx", None, None)
    return jax.shard_map(
        local, mesh=mesh,
        in_specs=(block, block, block, block, P("dp", None), P(), P()),
        out_specs=(block, block, block, block, P(), P()),
        check_vma=False,
    )
```

```python
import jax
import jax.numpy as jnp
from jax import lax
from jax.experimental import pallas as pl
from jax.experimental.pallas import tpu as pltpu
from jax.sharding import PartitionSpec as P

LOOKBACK_TOKENS = 1024
BLOCK = 256
WIDTH = 128
SPAN = 6
score_scale = 168.0 ** (-0.5)
log2_scale = score_scale * 1.4426950408889634
eps = 1e-06
HIDDEN = -1e30
CHIPS_ALONG_Z = 8
AHEAD = 2

MESH = pl.DeviceIdType.MESH
NT = (((1,), (1,)), ((), ()))
TN = (((0,), (0,)), ((), ()))
NN = (((1,), (0,)), ((), ()))


def dot(a, b, dims):
    return lax.dot_general(a, b, dims, preferred_element_type=jnp.float32)


def rows(block):
    return pl.ds(pl.multiple_of(block * BLOCK, BLOCK), BLOCK)


def normalize(raw, gain):
    wide = raw.astype(jnp.float32)
    factor = lax.rsqrt(jnp.mean(wide * wide, axis=-1, keepdims=True) + eps)
    unit = wide * factor
    return unit, factor, (unit * gain).astype(jnp.bfloat16)


def norm_backward(grad, unit, factor, gain):
    scaled = grad * gain
    inner = jnp.mean(scaled * unit, axis=-1, keepdims=True)
    return (factor * (scaled - unit * inner)).astype(jnp.bfloat16), jnp.sum(
        grad * unit, axis=0, keepdims=True
    )


def kernel(
    q_hbm, k_hbm, v_hbm, g_hbm, seg_ref, gain_q, gain_k,
    o_hbm, dq_hbm, dk_hbm, dv_hbm, total_ref,
    q_in, k_in, v_in, g_in, wide, q_own, g_own,
    kv, q_all, g_all, mask, s_buf, d_buf, p_bf, ds_bf, key_own, o_buf, dq_buf,
    o_in, dq_in, held, pair_out, pair_in, a_out, a_in, b_out, b_in,
    o_wide, dq_wide, dk_wide, dv_wide, part, part_in, z_part, x_part, y_part,
    local_sem, one_send, one_recv, sends, recvs, sum_send, sum_recv,
):
    dp = lax.axis_index("dp")
    me = lax.axis_index("ctx")
    count = lax.axis_size("ctx")
    line = 2 * CHIPS_ALONG_Z
    columns_of_x = count // line
    sequences = lax.axis_size("dp")
    core = lax.rem(me, 2)
    other = 1 - core
    chip = me // 2
    z_at = lax.rem(chip, CHIPS_ALONG_Z)
    x_at = me // line
    sibling = (dp, me + 1 - 2 * core)
    after = (dp, lax.rem(me + 2, count))
    before = (dp, lax.rem(me + count - 2, count))
    heads = kv.shape[0]
    first = jnp.where(chip == 0, 1, 0)
    last = jnp.where(chip == count // 2 - 1, 1, 0)

    def unless(flag, act):
        pl.when(flag == 0)(act)

    def along_z(d):
        return (dp, x_at * line + 2 * lax.rem(z_at + d, CHIPS_ALONG_Z) + core)

    def along_x(d):
        return (dp, lax.rem(me + d * line, count))

    def along_y(d):
        return (lax.rem(dp + d, sequences), me)

    barrier = pltpu.get_barrier_semaphore()
    friends = [sibling]
    friends += [along_z(d) for d in range(1, CHIPS_ALONG_Z)]
    friends += [along_x(d) for d in range(1, columns_of_x)]
    friends += [along_y(d) for d in range(1, sequences)]
    for device in friends:
        pl.semaphore_signal(barrier, inc=1, device_id=device, device_id_type=MESH)

    @pl.when(last == 0)
    def _():
        pl.semaphore_signal(barrier, inc=1, device_id=after, device_id_type=MESH)

    @pl.when(first == 0)
    def _():
        pl.semaphore_signal(barrier, inc=1, device_id=before, device_id_type=MESH)

    loads = [
        pltpu.make_async_copy(src, dst, local_sem.at[i])
        for i, (src, dst) in enumerate(
            ((k_hbm, k_in), (v_hbm, v_in), (q_hbm, q_in), (g_hbm, g_in))
        )
    ]
    for load in loads:
        load.start()

    def remote(src, dst, kind, head, device):
        return pltpu.make_async_remote_copy(
            src_ref=src, dst_ref=dst, send_sem=sends.at[kind, head], recv_sem=recvs.at[kind, head],
            device_id=device, device_id_type=MESH,
        )

    def own_to_after(h):
        return remote(kv.at[h, :, rows(4 + core)], kv.at[h, :, rows(2 + core)], 0, h, after)

    def pass_on(h):
        return remote(kv.at[h, :, rows(2 + core)], kv.at[h, :, rows(core)], 1, h, after)

    def share_near(h):
        return remote(kv.at[h, :, rows(2 + core)], kv.at[h, :, rows(2 + core)], 2, h, sibling)

    def share_far(h):
        return remote(kv.at[h, :, rows(core)], kv.at[h, :, rows(core)], 3, h, sibling)

    def output_to_sibling(h):
        return remote(o_buf.at[h, other], o_in.at[h], 4, h, sibling)

    def dquery_to_sibling(h):
        return remote(dq_buf.at[h, other], dq_in.at[h], 5, h, sibling)

    def terms_to_sibling(h):
        return remote(pair_out.at[h], pair_in.at[h], 6, h, sibling)

    def far_terms(h, side):
        return remote(a_out.at[h, side], a_in.at[h, side], 7 + side, h, before)

    def near_terms(h, side):
        return remote(b_out.at[h, side], b_in.at[h, side], 9 + side, h, before)

    def single(src, dst, index):
        return pltpu.make_async_remote_copy(
            src_ref=src, dst_ref=dst, send_sem=one_send.at[index], recv_sem=one_recv.at[index],
            device_id=sibling, device_id_type=MESH,
        )

    own_to_sibling = single(kv.at[:, :, rows(4 + core)], kv.at[:, :, rows(4 + core)], 0)
    query_to_sibling = single(q_own.at[:, other], q_all.at[:, rows(core)], 1)
    grad_to_sibling = single(g_own.at[:, other], g_all.at[:, rows(core)], 2)
    part_to_sibling = single(part, part_in, 3)

    def spread(ref, slot, index, device):
        return pltpu.make_async_remote_copy(
            src_ref=ref.at[slot], dst_ref=ref.at[slot],
            send_sem=sum_send.at[index], recv_sem=sum_recv.at[index],
            device_id=device, device_id_type=MESH,
        )

    z_sums = [spread(z_part, z_at, d, along_z(d)) for d in range(1, CHIPS_ALONG_Z)]
    x_sums = [
        spread(x_part, x_at, CHIPS_ALONG_Z + d, along_x(d)) for d in range(1, columns_of_x)
    ]
    y_sums = [
        spread(y_part, dp, CHIPS_ALONG_Z + columns_of_x + d, along_y(d))
        for d in range(1, sequences)
    ]
    query_gain = gain_q[...]
    key_gain = gain_k[...]

    def widen(ref):
        tokens, across, width = ref.shape
        wide[pl.ds(0, tokens * across)] = (
            ref[...].astype(jnp.float32).reshape(tokens * across, width)
        )

    def head_of(h, across):
        return wide[pl.ds(h, BLOCK, stride=across)].astype(jnp.bfloat16)

    loads[0].wait()
    widen(k_in)
    for h in range(heads):
        key_own[h] = head_of(h, heads)
        kv[h, 0, rows(4 + core)] = normalize(key_own[h], key_gain)[2]
    loads[1].wait()
    widen(v_in)
    for h in range(heads):
        kv[h, 1, rows(4 + core)] = head_of(h, heads)

    pl.semaphore_wait(barrier, len(friends) + 2 - first - last)

    for h in range(AHEAD):
        unless(last, own_to_after(h).start)
    own_to_sibling.start()

    for load, source, own, everything, copy in (
        (loads[2], q_in, q_own, q_all, query_to_sibling),
        (loads[3], g_in, g_own, g_all, grad_to_sibling),
    ):
        load.wait()
        widen(source)
        for h in range(heads):
            for pair in range(2):
                own[h, pair] = head_of(2 * h + pair, 2 * heads)
        copy.start()
        for h in range(heads):
            everything[h, rows(core)] = own[h, core]

    part[...] = jnp.zeros_like(part)

    @pl.when(first == 1)
    def _():
        nothing = jnp.zeros((2, BLOCK, WIDTH), jnp.bfloat16)
        for h in range(heads):
            kv[h, :, rows(core)] = nothing
            kv[h, :, rows(2 + core)] = nothing

    @pl.when(last == 1)
    def _():
        a_in[...] = jnp.zeros_like(a_in)
        b_in[...] = jnp.zeros_like(b_in)

    corner = jnp.zeros((BLOCK, BLOCK), jnp.bfloat16)
    for ref in (p_bf, ds_bf):
        ref[pl.ds(0, BLOCK), pl.ds(BLOCK, BLOCK)] = corner
        ref[pl.ds(5 * BLOCK, BLOCK), pl.ds(0, BLOCK)] = corner

    def arrive_near(h):
        unless(first, own_to_after(h).wait_recv)
        unless(last, pass_on(h).start)
        share_near(h).start()

    arrive_near(0)
    unless(last, own_to_after(AHEAD).start)

    def segments_of(block):
        place = jnp.maximum(2 * chip - 4 + block, 0) * BLOCK
        found = seg_ref[0:1, pl.ds(pl.multiple_of(place, BLOCK), BLOCK)].astype(jnp.float32)
        return jnp.where(2 * chip - 4 + block >= 0, found, -1.0)

    for kb in range(SPAN):
        by_key = jnp.broadcast_to(segments_of(kb), (WIDTH, BLOCK)).T
        for qb in range(2):
            if not qb <= kb < qb + 5:
                continue
            by_query = segments_of(4 + qb)
            for part_at in range(0, BLOCK, WIDTH):
                behind = (
                    (4 + qb - kb) * BLOCK
                    + part_at
                    + lax.broadcasted_iota(jnp.int32, (BLOCK, WIDTH), 1)
                    - lax.broadcasted_iota(jnp.int32, (BLOCK, WIDTH), 0)
                )
                allowed = (
                    (behind >= 0)
                    & (behind < LOOKBACK_TOKENS)
                    & (by_key == by_query[:, part_at : part_at + WIDTH])
                )
                mask[pl.ds(kb * BLOCK, BLOCK), pl.ds(qb * BLOCK + part_at, WIDTH)] = jnp.where(
                    allowed, 0.0, HIDDEN
                )

    for h in range(1, AHEAD):
        arrive_near(h)
        unless(last, own_to_after(h + AHEAD).start)
    own_to_sibling.wait_recv()
    query_to_sibling.wait_recv()
    grad_to_sibling.wait_recv()

    def attend(h):
        query_unit, query_factor, query_normed = normalize(q_all[h], query_gain)
        grad = g_all[h]
        for qb in range(2):
            columns = slice(qb * BLOCK, (qb + 1) * BLOCK)
            top = None
            for i in range(5):
                kb = pl.ds((qb + i) * BLOCK, BLOCK)
                scores = dot(kv[h, 0, kb], query_normed[columns], NT) * log2_scale + mask[kb, columns]
                s_buf[qb, i] = scores
                tile_top = jnp.max(scores, axis=0, keepdims=True)
                top = tile_top if top is None else jnp.maximum(top, tile_top)
            total = jnp.zeros((1, BLOCK), jnp.float32)
            inner = jnp.zeros((1, BLOCK), jnp.float32)
            for i in range(5):
                kb = pl.ds((qb + i) * BLOCK, BLOCK)
                dprob = dot(kv[h, 1, kb], grad[columns], NT)
                weight = jnp.exp2(s_buf[qb, i] - top)
                s_buf[qb, i] = weight
                d_buf[qb, i] = dprob
                total = total + jnp.sum(weight, axis=0, keepdims=True)
                inner = inner + jnp.sum(weight * dprob, axis=0, keepdims=True)
            inverse = 1.0 / total
            delta = inner * inverse
            for i in range(5):
                kb = pl.ds((qb + i) * BLOCK, BLOCK)
                probs = s_buf[qb, i] * inverse
                p_bf[kb, columns] = probs.astype(jnp.bfloat16)
                ds_bf[kb, columns] = (probs * (d_buf[qb, i] - delta)).astype(jnp.bfloat16)
        key_part = jnp.zeros((1, WIDTH), jnp.float32)
        for near in range(3):
            kb = rows(2 * near + other)
            dkey = dot(ds_bf[kb], query_normed, NN) * score_scale
            pair_out[h, near, 0] = dkey.astype(jnp.bfloat16)
            pair_out[h, near, 1] = dot(p_bf[kb], grad, NN).astype(jnp.bfloat16)
            key_part = key_part + jnp.sum(
                dkey * kv[h, 0, kb].astype(jnp.float32), axis=0, keepdims=True
            )
        terms_to_sibling(h).start()
        for near in range(3):
            kb = rows(2 * near + core)
            dkey = dot(ds_bf[kb], query_normed, NN) * score_scale
            held[h, near, 0] = dkey
            held[h, near, 1] = dot(p_bf[kb], grad, NN)
            key_part = key_part + jnp.sum(
                dkey * kv[h, 0, kb].astype(jnp.float32), axis=0, keepdims=True
            )
        query_part = jnp.zeros((1, WIDTH), jnp.float32)
        for qb in range(2):
            columns = slice(qb * BLOCK, (qb + 1) * BLOCK)
            window = pl.ds(qb * BLOCK, 5 * BLOCK)
            dquery = dot(kv[h, 0, window], ds_bf[window, columns], TN).T * score_scale
            dq_buf[h, qb], gain_part = norm_backward(
                dquery, query_unit[columns], query_factor[columns], query_gain
            )
            query_part = query_part + gain_part
            o_buf[h, qb] = dot(kv[h, 1, window], p_bf[window, columns], TN).T.astype(jnp.bfloat16)
        part[0:1] += query_part
        part[1:2] += key_part / key_gain
        dquery_to_sibling(h).start()
        output_to_sibling(h).start()

    def send_far(h):
        terms_to_sibling(h).wait_recv()
        for side in range(2):
            a_out[h, side] = (
                held[h, 0, side] + pair_in[h, 0, side].astype(jnp.float32)
            ).astype(jnp.bfloat16)
            unless(first, far_terms(h, side).start)

    def send_near(h):
        for side in range(2):
            unless(last, far_terms(h, side).wait_recv)
            b_out[h, side] = (
                held[h, 1, side]
                + pair_in[h, 1, side].astype(jnp.float32)
                + a_in[h, side].astype(jnp.float32)
            ).astype(jnp.bfloat16)
            unless(first, near_terms(h, side).start)

    def finish_key(h):
        terms = []
        for side in range(2):
            unless(last, near_terms(h, side).wait_recv)
            terms.append(
                held[h, 2, side]
                + pair_in[h, 2, side].astype(jnp.float32)
                + b_in[h, side].astype(jnp.float32)
            )
        unit, factor, _ = normalize(key_own[h], key_gain)
        grad, _ = norm_backward(terms[0], unit, factor, key_gain)
        dk_wide[pl.ds(h, BLOCK, stride=heads)] = grad.astype(jnp.float32)
        dv_wide[pl.ds(h, BLOCK, stride=heads)] = terms[1]

    def step(s, carry):
        share_near(s).wait_recv()
        share_far(s).wait_recv()
        attend(s)

        @pl.when(s == heads - 1)
        def _():
            x_part[x_at] = part[...]
            for copy in x_sums:
                copy.start()

        send_far(s)

        @pl.when(s + AHEAD < heads)
        def _():
            arrive_near(s + AHEAD)

        @pl.when((s + 2 * AHEAD < heads) & (last == 0))
        def _():
            own_to_after(s + 2 * AHEAD).start()

        @pl.when(s + 1 < heads)
        def _():
            unless(first, pass_on(s + 1).wait_recv)
            share_far(s + 1).start()

        @pl.when(s >= 1)
        def _():
            send_near(s - 1)

        @pl.when(s >= 2)
        def _():
            finish_key(s - 2)

        return carry

    unless(first, pass_on(0).wait_recv)
    share_far(0).start()
    lax.fori_loop(0, heads, step, 0)

    def natural(into, ours, theirs, h):
        into[pl.ds(2 * h + core, BLOCK, stride=2 * heads)] = ours[h, core].astype(jnp.float32)
        into[pl.ds(2 * h + other, BLOCK, stride=2 * heads)] = theirs[h].astype(jnp.float32)

    def narrow(into, ref):
        tokens, across, width = into.shape
        into[...] = ref[...].reshape(tokens, across, width).astype(jnp.bfloat16)

    for copy in x_sums:
        copy.wait_recv()
    y_part[dp] = jnp.sum(x_part[...], axis=0)
    for copy in y_sums:
        copy.start()
    for h in range(heads):
        dquery_to_sibling(h).wait_recv()
        natural(dq_wide, dq_buf, dq_in, h)
    for copy in y_sums:
        copy.wait_recv()
    part[...] = jnp.sum(y_part[...], axis=0)
    part_to_sibling.start()
    narrow(q_in, dq_wide)
    stores = [pltpu.make_async_copy(q_in, dq_hbm, local_sem.at[0])]
    stores[0].start()
    part_to_sibling.wait_recv()
    z_part[z_at] = part[...] + part_in[...]
    for copy in z_sums:
        copy.start()
    send_near(heads - 1)
    for h in range(heads):
        output_to_sibling(h).wait_recv()
        natural(o_wide, o_buf, o_in, h)
    narrow(g_in, o_wide)
    stores.append(pltpu.make_async_copy(g_in, o_hbm, local_sem.at[1]))
    stores[1].start()
    finish_key(heads - 2)
    finish_key(heads - 1)
    narrow(k_in, dk_wide)
    stores.append(pltpu.make_async_copy(k_in, dk_hbm, local_sem.at[2]))
    stores[2].start()
    narrow(v_in, dv_wide)
    stores.append(pltpu.make_async_copy(v_in, dv_hbm, local_sem.at[3]))
    stores[3].start()
    for copy in z_sums:
        copy.wait_recv()
    total_ref[...] = jnp.sum(z_part[...], axis=0)

    def sent(h, carry):
        for copy in (
            share_near, share_far, output_to_sibling, dquery_to_sibling, terms_to_sibling,
        ):
            copy(h).wait_send()
        for copy in (own_to_after(h), pass_on(h)):
            unless(last, copy.wait_send)
        for side in range(2):
            unless(first, far_terms(h, side).wait_send)
            unless(first, near_terms(h, side).wait_send)
        return carry

    lax.fori_loop(0, heads, sent, 0)
    for copy in (own_to_sibling, query_to_sibling, grad_to_sibling, part_to_sibling):
        copy.wait_send()
    for copy in z_sums + x_sums + y_sums:
        copy.wait_send()
    for store in stores:
        store.wait()


def attention(q, k, v, g, segments, gain_q, gain_k, sequences, columns_of_x):
    tokens, groups, width = k.shape
    half = jnp.bfloat16
    wide = jnp.float32
    vmem = pl.BlockSpec(memory_space=pltpu.VMEM)
    anywhere = pl.BlockSpec(memory_space=pl.ANY)
    dma = pltpu.SemaphoreType.DMA
    sums = CHIPS_ALONG_Z + columns_of_x + sequences
    return pl.pallas_call(
        kernel,
        out_shape=[
            jax.ShapeDtypeStruct(q.shape, half),
            jax.ShapeDtypeStruct(q.shape, half),
            jax.ShapeDtypeStruct(k.shape, half),
            jax.ShapeDtypeStruct(k.shape, half),
            jax.ShapeDtypeStruct((8, width), wide),
        ],
        in_specs=[anywhere] * 4 + [vmem] * 3,
        out_specs=[anywhere] * 4 + [vmem],
        scratch_shapes=[
            pltpu.VMEM(q.shape, half),
            pltpu.VMEM(k.shape, half),
            pltpu.VMEM(k.shape, half),
            pltpu.VMEM(q.shape, half),
            pltpu.VMEM((2 * groups * tokens, width), wide),
            pltpu.VMEM((groups, 2, tokens, width), half),
            pltpu.VMEM((groups, 2, tokens, width), half),
            pltpu.VMEM((groups, 2, SPAN * tokens, width), half),
            pltpu.VMEM((groups, 2 * tokens, width), half),
            pltpu.VMEM((groups, 2 * tokens, width), half),
            pltpu.VMEM((SPAN * tokens, 2 * tokens), wide),
            pltpu.VMEM((2, 5, tokens, tokens), wide),
            pltpu.VMEM((2, 5, tokens, tokens), wide),
            pltpu.VMEM((SPAN * tokens, 2 * tokens), half),
            pltpu.VMEM((SPAN * tokens, 2 * tokens), half),
            pltpu.VMEM((groups, tokens, width), half),
            pltpu.VMEM((groups, 2, tokens, width), half),
            pltpu.VMEM((groups, 2, tokens, width), half),
            pltpu.VMEM((groups, tokens, width), half),
            pltpu.VMEM((groups, tokens, width), half),
            pltpu.VMEM((groups, 3, 2, tokens, width), wide),
            pltpu.VMEM((groups, 3, 2, tokens, width), half),
            pltpu.VMEM((groups, 3, 2, tokens, width), half),
            pltpu.VMEM((groups, 2, tokens, width), half),
            pltpu.VMEM((groups, 2, tokens, width), half),
            pltpu.VMEM((groups, 2, tokens, width), half),
            pltpu.VMEM((groups, 2, tokens, width), half),
            pltpu.VMEM((2 * groups * tokens, width), wide),
            pltpu.VMEM((2 * groups * tokens, width), wide),
            pltpu.VMEM((groups * tokens, width), wide),
            pltpu.VMEM((groups * tokens, width), wide),
            pltpu.VMEM((8, width), wide),
            pltpu.VMEM((8, width), wide),
            pltpu.VMEM((CHIPS_ALONG_Z, 8, width), wide),
            pltpu.VMEM((columns_of_x, 8, width), wide),
            pltpu.VMEM((sequences, 8, width), wide),
            dma((4,)),
            dma((4,)),
            dma((4,)),
            dma((11, groups)),
            dma((11, groups)),
            dma((sums,)),
            dma((sums,)),
        ],
        compiler_params=pltpu.CompilerParams(
            collective_id=0, has_side_effects=True, vmem_limit_bytes=60 * 2**20
        ),
        name="attention",
    )(q, k, v, g, segments, gain_q, gain_k)


def deliver_kernel(
    o, dq, dk, dv, total, o_out, dq_out, dk_out, dv_out, gain_q, gain_k,
    o_held, dq_held, dk_held, dv_held, load_sem, store_sem,
):
    loads = []
    stores = []
    for src, held, dst, pieces in (
        (o, o_held, o_out, 4), (dq, dq_held, dq_out, 4),
        (dk, dk_held, dk_out, 2), (dv, dv_held, dv_out, 2),
    ):
        size = src.shape[0] // pieces
        for piece in range(pieces):
            span = pl.ds(piece * size, size)
            at = len(loads)
            loads.append(pltpu.make_async_copy(src.at[span], held.at[span], load_sem.at[at]))
            stores.append(pltpu.make_async_copy(held.at[span], dst.at[span], store_sem.at[at]))
    for load in loads:
        load.start()
    gain_q[...] = total[0:1]
    gain_k[...] = total[1:2]
    for load, store in zip(loads, stores):
        load.wait()
        store.start()
    for store in stores:
        store.wait()


def deliver(output, query_grad, key_grad, value_grad, total):
    vmem = pl.BlockSpec(memory_space=pltpu.VMEM)
    anywhere = pl.BlockSpec(memory_space=pl.ANY)
    arrays = (output, query_grad, key_grad, value_grad)
    gain = jax.ShapeDtypeStruct((1, total.shape[1]), total.dtype)
    return pl.pallas_call(
        deliver_kernel,
        out_shape=[jax.ShapeDtypeStruct(array.shape, array.dtype) for array in arrays] + [gain] * 2,
        in_specs=[anywhere] * 4 + [vmem],
        out_specs=[anywhere] * 4 + [vmem] * 2,
        scratch_shapes=[pltpu.VMEM(array.shape, array.dtype) for array in arrays]
        + [pltpu.SemaphoreType.DMA((12,))] * 2,
        name="deliver",
    )(*arrays, total)


def local(queries, keys, values, out_grad, segment_ids, query_gain, key_gain):
    sequences = lax.axis_size("dp")
    columns_of_x = lax.axis_size("ctx") // (2 * CHIPS_ALONG_Z)
    results = attention(
        queries[0], keys[0], values[0], out_grad[0], segment_ids,
        query_gain[None], key_gain[None], sequences, columns_of_x,
    )
    output, query_grad, key_grad, value_grad, query_total, key_total = deliver(*results)
    return (
        output[None], query_grad[None], key_grad[None], value_grad[None],
        query_total[0], key_total[0],
    )


def solution(mesh):
    block = P("dp", "ctx", None, None)
    return jax.shard_map(
        local, mesh=mesh,
        in_specs=(block, block, block, block, P("dp", None), P(), P()),
        out_specs=(block, block, block, block, P(), P()),
        check_vma=False,
    )
```
